256 devices in a mesh: dp: 2 (over y_hi), row: 32 (over y_lo, z, core), chan: 4 (over x).
Axes of the slice: x: 4, y: 4 (y_hi: 2, y_lo: 2; y = y_hi * 2 + y_lo), z: 8, core: 2. Of those that a mesh axis runs over, the one named last changes fastest.
Arguments:
- pair_rep: bfloat16 [2048, 1024, 128], P(('dp', 'row', 'chan')), parts along dimension 0, may hold values from -16 to 16
- token_mask: int32 [2048], P('dp'), parts along dimension 0, may hold values from 0 to 1, as said below
- w_a_gate: bfloat16 [128, 128], replicated, may hold values from -0.5 to 0.5
- w_a_proj: bfloat16 [128, 128], replicated, may hold values from -0.5 to 0.5
- w_b_gate: bfloat16 [128, 128], replicated, may hold values from -0.5 to 0.5
- w_b_proj: bfloat16 [128, 128], replicated, may hold values from -0.5 to 0.5
- w_gate: bfloat16 [128, 128], replicated, may hold values from -0.5 to 0.5
- w_out: bfloat16 [128, 128], replicated, may hold values from -0.5 to 0.5
- w_dist: bfloat16 [128, 64], replicated, may hold values from -0.5 to 0.5
Outputs:
- updated_pair: bfloat16 [2048, 1024, 128], P(('dp', 'row', 'chan')), parts along dimension 0
- dist_logits: float32 [64, 2048, 1024], P(None, ('dp', 'row', 'chan')), parts along dimension 1
The draws below stay inside these ranges and needn't reach their ends.
There are 2 independent parts, one for each index of `dp`. The reference program is written for one: setup_inputs(seed, part) draws one part's arguments, and reference() takes and returns one part's arrays. A program takes and returns all parts, laid end to end along the dimension named above; an argument that names none is the same for every part. Nothing has to cross between parts.
Inputs may be any that keep to these rules, and one draw needn't show every extreme that they name: `token_mask`: the first token is 1 and the last is 0; tokens between may be 0.
All inputs are finite; a program needn't handle non-finite values.
Results may differ from the reference program's by a relative error of at most 0.0049.
Values may be sent and summed in bfloat16 or wider, within the bound.
No kernel may reach another device: no remote copies, remote signals or barrier semaphores. Data moves between devices by JAX's collectives and lax.ppermute only.
A program may use at most 128 MiB of HBM per device.

```python
import math
import jax
import jax.numpy as jnp
from jax import lax

C = 128
H = 128
BINS = 64
N = 1024


def draw_pair_rep(key, part):
    key = jax.random.fold_in(key, 11)
    key_noise, key_chan = jax.random.split(key, 2)
    chan_scale = jnp.exp(jax.random.uniform(key_chan, (C,), minval=-1.0, maxval=1.0))
    noise = jnp.clip(jax.random.normal(key_noise, (N, N, C)), -4.0, 4.0)
    field = noise * chan_scale
    return field.astype(jnp.float32).astype(jnp.bfloat16)


def draw_token_mask(key, part):
    key = jax.random.fold_in(key, 23)
    key_length, key_gaps = jax.random.split(key)
    length = jax.random.randint(key_length, (), N // 2, N)
    positions = jnp.arange(N, dtype=jnp.int32)
    resolved = (jax.random.randint(key_gaps, (N,), 0, 8) != 0).astype(jnp.int32)
    resolved = jnp.where(positions == 0, 1, resolved)
    return (positions < length).astype(jnp.int32) * resolved


def gaussian(key, shape, spread, reach, kind=jnp.bfloat16):
    result = jax.random.normal(key, shape, jnp.float32) * spread
    return jnp.minimum(jnp.maximum(result, -reach), reach).astype(kind)


def setup_inputs(seed: int = 0, part: int = 0) -> dict:
    key_list = jax.random.split(jax.random.key(seed), 10)
    own_keys = jax.random.split(jax.random.fold_in(key_list[9], part), 10)
    pair_rep = draw_pair_rep(jax.random.fold_in(jax.random.fold_in(key_list[9], part), 71), part)
    token_mask = draw_token_mask(jax.random.fold_in(jax.random.fold_in(key_list[9], part), 71), part)
    w_a_gate = gaussian(key_list[2], (C, H), C ** -0.5, 0.5)
    w_a_proj = gaussian(key_list[3], (C, H), C ** -0.5, 0.5)
    w_b_gate = gaussian(key_list[4], (C, H), C ** -0.5, 0.5)
    w_b_proj = gaussian(key_list[5], (C, H), C ** -0.5, 0.5)
    w_gate = gaussian(key_list[6], (C, C), C ** -0.5, 0.5)
    w_out = gaussian(key_list[7], (H, C), H ** -0.5, 0.5)
    w_dist = gaussian(key_list[8], (C, BINS), C ** -0.5, 0.5)
    return dict(pair_rep=pair_rep, token_mask=token_mask, w_a_gate=w_a_gate, w_a_proj=w_a_proj, w_b_gate=w_b_gate, w_b_proj=w_b_proj, w_gate=w_gate, w_out=w_out, w_dist=w_dist)


epsilon = 1e-05

def layer_norm(values, axis_index):
    values = values.astype(jnp.float32)
    center = values - lax.optimization_barrier(jnp.mean(values, axis=axis_index, keepdims=True))
    second = lax.optimization_barrier(jnp.mean(center * center, axis=axis_index, keepdims=True))
    return center * lax.rsqrt(second + epsilon)

def reference(pair_rep, token_mask, w_a_gate, w_a_proj, w_b_gate, w_b_proj, w_gate, w_out, w_dist):
    normed = layer_norm(pair_rep, 2).astype(jnp.bfloat16)
    present = token_mask.astype(jnp.float32)
    pair_keep = present[:, None] * present[None, :]
    flat_normed = normed.reshape(N * N, C)
    group_size = 8

    def stack_cols(weight):
        return jnp.transpose(weight.reshape(C, H // group_size, group_size), (1, 0, 2))

    def channel_group(weights):
        w_ag, w_ap, w_bg, w_bp = weights

        def gated(w_first, w_second):
            gate_part = jnp.dot(flat_normed, w_first, preferred_element_type=jnp.float32)
            proj_part = jnp.dot(flat_normed, w_second, preferred_element_type=jnp.float32)
            values = (jax.nn.sigmoid(gate_part) * proj_part).reshape(N, N, group_size) * pair_keep[:, :, None]
            return jnp.transpose(values, (2, 0, 1)).astype(jnp.bfloat16)
        left_side = gated(w_ag, w_ap)
        right_side = gated(w_bg, w_bp)
        summed = jnp.einsum('hki,hkj->hij', left_side.astype(jnp.float32), right_side.astype(jnp.float32))
        return summed.astype(jnp.bfloat16)
    product = lax.map(channel_group, (stack_cols(w_a_gate), stack_cols(w_a_proj), stack_cols(w_b_gate), stack_cols(w_b_proj)))
    product = product.reshape(H, N, N)
    block_rows = math.gcd(N, 128)

    def finish_block(index):
        begin = index * block_rows
        out_rows = lax.dynamic_slice_in_dim(product, begin, block_rows, 1)
        normed_rows = lax.dynamic_slice_in_dim(normed, begin, block_rows, 0)
        base_rows = lax.dynamic_slice_in_dim(pair_rep, begin, block_rows, 0)
        gate_vals = jax.nn.sigmoid(jnp.dot(normed_rows.reshape(-1, C), w_gate, preferred_element_type=jnp.float32)).reshape(block_rows, N, C)
        normal_out = layer_norm(out_rows, 0).astype(jnp.bfloat16)
        projected = jnp.einsum('hij,hc->ijc', normal_out.astype(jnp.float32), w_out.astype(jnp.float32))
        return (base_rows.astype(jnp.float32) + gate_vals * projected).astype(jnp.bfloat16)
    updated = lax.map(finish_block, jnp.arange(N // block_rows, dtype=jnp.int32)).reshape(N, N, C)
    own_logits = jnp.dot(updated.reshape(N * N, C), w_dist, preferred_element_type=jnp.float32).reshape(N, N, BINS)
    logits = own_logits + jnp.transpose(own_logits, (1, 0, 2))
    return (updated, jnp.transpose(logits, (2, 0, 1)))
```

```python
import jax
import jax.numpy as jnp
from jax import lax
from jax.experimental import pallas as pl
from jax.experimental.pallas import tpu as pltpu
from jax.sharding import PartitionSpec as P

EPS = 1e-05
GROUP = ("row", "chan")
ROWS = 8
LANES = 128
VMEM_LIMIT = 48 * 1024 * 1024

F32 = jnp.float32
BF16 = jnp.bfloat16


def params():
    return pltpu.CompilerParams(vmem_limit_bytes=VMEM_LIMIT)


def sides_kernel(own_ref, mask_ref, x_ref, wag_ref, wap_ref, wbg_ref, wbp_ref, normed_ref, sides_ref, scratch):
    rows, wide, channels = x_ref.shape
    x = x_ref[...].astype(F32).reshape(rows * wide, channels)
    center = x - jnp.mean(x, axis=1, keepdims=True)
    second = jnp.mean(center * center, axis=1, keepdims=True)
    normed = (center * lax.rsqrt(second + EPS)).astype(BF16)
    normed_ref[...] = normed.reshape(x_ref.shape)
    mask = mask_ref[0].astype(F32)
    for side, (gate_ref, proj_ref) in enumerate(((wag_ref, wap_ref), (wbg_ref, wbp_ref))):
        gate = lax.dot_general(gate_ref[...], normed, (((0,), (1,)), ((), ())), preferred_element_type=F32)
        proj = lax.dot_general(proj_ref[...], normed, (((0,), (1,)), ((), ())), preferred_element_type=F32)
        both = jax.nn.sigmoid(gate) * proj
        for k in range(rows):
            keep = mask * own_ref[k].astype(F32)
            scratch[pl.ds(k, LANES, stride=rows), :] = both[:, k * wide : (k + 1) * wide] * keep
        sides_ref[:, side] = scratch[...].reshape(LANES, rows, wide).astype(BF16)


def make_sides(pair_rep, own_mask, token_mask, w_a_gate, w_a_proj, w_b_gate, w_b_proj):
    rows, columns, channels = pair_rep.shape
    steps = columns // LANES
    weight = pl.BlockSpec((channels, LANES), lambda g: (0, 0))
    return pl.pallas_call(
        sides_kernel,
        grid=(steps,),
        in_specs=[
            pl.BlockSpec(memory_space=pltpu.SMEM),
            pl.BlockSpec((1, 1, LANES), lambda g: (g, 0, 0)),
            pl.BlockSpec((rows, LANES, channels), lambda g: (0, g, 0)),
            weight,
            weight,
            weight,
            weight,
        ],
        out_specs=[
            pl.BlockSpec((rows, LANES, channels), lambda g: (0, g, 0)),
            pl.BlockSpec((LANES, 2, rows, LANES), lambda g: (0, 0, 0, g)),
        ],
        out_shape=[
            jax.ShapeDtypeStruct(pair_rep.shape, BF16),
            jax.ShapeDtypeStruct((LANES, 2, rows, columns), BF16),
        ],
        scratch_shapes=[pltpu.VMEM((rows * LANES, LANES), F32)],
        compiler_params=params(),
        name="sides",
    )(own_mask, token_mask.reshape(steps, 1, LANES), pair_rep, w_a_gate, w_a_proj, w_b_gate, w_b_proj)


def product_kernel(left_ref, right_ref, out_ref):
    depth = right_ref.shape[0] * right_ref.shape[2]
    left = left_ref[:, 0].reshape(depth, left_ref.shape[3])
    right = right_ref[:, 0].reshape(depth, right_ref.shape[3])
    prod = lax.dot_general(left, right, (((0,), (0,)), ((), ())), preferred_element_type=F32)
    out_ref[...] = prod.reshape(out_ref.shape).astype(BF16)


def make_product(sides):
    sources, _, rows, columns = sides.shape
    block = 256
    return pl.pallas_call(
        product_kernel,
        grid=(columns // block,),
        in_specs=[
            pl.BlockSpec((sources, 1, rows, block), lambda g: (0, 0, 0, g)),
            pl.BlockSpec((sources, 1, rows, columns), lambda g: (0, 1, 0, 0)),
        ],
        out_specs=pl.BlockSpec((block // rows, rows, columns), lambda g: (g, 0, 0)),
        out_shape=jax.ShapeDtypeStruct((columns // rows, rows, columns), BF16),
        compiler_params=params(),
        name="product",
    )(sides, sides)


def finish_kernel(
    x_ref, base_ref, normed_ref, wg_ref, wo_ref, wd_ref, w8_ref, upd_ref, own_ref, mirror_ref, scratch, wide_ref, stage
):
    rows, wide, channels = base_ref.shape
    owners = wide // rows
    bins = wd_ref.shape[1]
    x = x_ref[...].astype(F32)
    center = x - jnp.mean(x, axis=0, keepdims=True)
    second = jnp.mean(center * center, axis=0, keepdims=True)
    scratch[...] = (center * lax.rsqrt(second + EPS)).reshape(scratch.shape)
    tri = jnp.concatenate(
        [scratch[pl.ds(r, LANES, stride=rows), :].astype(BF16) for r in range(rows)], axis=1
    )
    projected = lax.dot_general(tri, wo_ref[...], (((0,), (0,)), ((), ())), preferred_element_type=F32)
    normed = normed_ref[...].reshape(rows * wide, channels)
    gate = jax.nn.sigmoid(jnp.dot(normed, wg_ref[...], preferred_element_type=F32))
    base = base_ref[...].reshape(rows * wide, channels).astype(F32)
    updated = (base + gate * projected).astype(BF16)
    upd_ref[...] = updated.reshape(upd_ref.shape)
    wide_ref[...] = updated.astype(F32)
    own = lax.dot_general(wd_ref[...], updated, (((0,), (1,)), ((), ())), preferred_element_type=F32)
    for r in range(rows):
        stage[pl.ds(r, bins, stride=rows), :] = own[:, r * wide : (r + 1) * wide]
    own_ref[...] = stage[...].reshape(own_ref.shape)
    picks = []
    for s in range(rows):
        parts = [wide_ref[pl.ds(d * rows + s, rows, stride=wide), :] for d in range(owners)]
        picks.append(jnp.concatenate(parts, axis=0).astype(BF16))
    mirror = jnp.dot(jnp.concatenate(picks, axis=1), w8_ref[...], preferred_element_type=F32)
    mirror_ref[...] = mirror.reshape(mirror_ref.shape).astype(BF16)


def make_finish(product, pair_rep, normed, w_gate, w_out, w_dist, w8):
    rows, columns, channels = pair_rep.shape
    bins = w_dist.shape[1]
    block = lambda g: (0, g, 0)
    fixed = lambda g: (0, 0)
    owners = LANES // rows
    return pl.pallas_call(
        finish_kernel,
        grid=(columns // LANES,),
        in_specs=[
            pl.BlockSpec((LANES, rows, LANES), lambda g: (0, 0, g)),
            pl.BlockSpec((rows, LANES, channels), block),
            pl.BlockSpec((rows, LANES, channels), block),
            pl.BlockSpec(w_gate.shape, fixed),
            pl.BlockSpec(w_out.shape, fixed),
            pl.BlockSpec(w_dist.shape, fixed),
            pl.BlockSpec(w8.shape, fixed),
        ],
        out_specs=[
            pl.BlockSpec((rows, LANES, channels), block),
            pl.BlockSpec((bins, rows, LANES), lambda g: (0, 0, g)),
            pl.BlockSpec((owners, rows, bins * rows), lambda g: (g, 0, 0)),
        ],
        out_shape=[
            jax.ShapeDtypeStruct(pair_rep.shape, BF16),
            jax.ShapeDtypeStruct((bins, rows, columns), F32),
            jax.ShapeDtypeStruct((columns // rows, rows, bins * rows), BF16),
        ],
        scratch_shapes=[
            pltpu.VMEM((LANES * rows, LANES), F32),
            pltpu.VMEM((rows * LANES, channels), F32),
            pltpu.VMEM((bins * rows, LANES), F32),
        ],
        compiler_params=params(),
        name="finish",
    )(product, pair_rep, normed, w_gate, w_out, w_dist, w8)


def add_kernel(own_ref, mirror_ref, out_ref):
    deep, rows, columns = own_ref.shape
    mirror = mirror_ref[...].reshape(columns, deep * rows)
    out_ref[...] = own_ref[...] + mirror.astype(F32).T.reshape(deep, rows, columns)


def make_add(own, mirror):
    bins, rows, columns = own.shape
    deep = LANES // rows
    return pl.pallas_call(
        add_kernel,
        grid=(bins // deep,),
        in_specs=[
            pl.BlockSpec((deep, rows, columns), lambda g: (g, 0, 0)),
            pl.BlockSpec((columns // rows, rows, LANES), lambda g: (0, 0, g)),
        ],
        out_specs=pl.BlockSpec((deep, rows, columns), lambda g: (g, 0, 0)),
        out_shape=jax.ShapeDtypeStruct(own.shape, F32),
        compiler_params=params(),
        name="add",
    )(own, mirror)


def exchange(values):
    return lax.all_to_all(values, GROUP, split_axis=0, concat_axis=0, tiled=True)


def spread_bins(w_dist):
    channels, bins = w_dist.shape
    repeated = jnp.repeat(w_dist, ROWS, axis=1)
    which = jnp.arange(bins * ROWS) % ROWS
    chosen = which[None, None, :] == jnp.arange(ROWS)[:, None, None]
    return jnp.where(chosen, repeated[None], jnp.zeros((), BF16)).reshape(ROWS * channels, bins * ROWS)


def local(pair_rep, token_mask, w_a_gate, w_a_proj, w_b_gate, w_b_proj, w_gate, w_out, w_dist):
    rows = pair_rep.shape[0]
    own_mask = lax.dynamic_slice_in_dim(token_mask, lax.axis_index(GROUP) * rows, rows)
    normed, sides = make_sides(pair_rep, own_mask, token_mask, w_a_gate, w_a_proj, w_b_gate, w_b_proj)
    sides = exchange(sides)
    product = exchange(make_product(sides))
    updated, own, mirror = make_finish(
        product, pair_rep, normed, w_gate, w_out, w_dist, spread_bins(w_dist)
    )
    logits = make_add(own, exchange(mirror))
    return (updated, logits)


def solution(mesh):
    in_specs = (P(("dp", "row", "chan"), None, None), P("dp"), P(), P(), P(), P(), P(), P(), P())
    out_specs = (P(("dp", "row", "chan"), None, None), P(None, ("dp", "row", "chan"), None))
    return jax.shard_map(local, mesh=mesh, in_specs=in_specs, out_specs=out_specs, check_vma=False)
```

```python
import jax
import jax.numpy as jnp
from jax import lax
from jax.experimental import pallas as pl
from jax.experimental.pallas import tpu as pltpu
from jax.sharding import PartitionSpec as P

EPS = 1e-05
GROUP = ("row", "chan")
ROWS = 8
LANES = 128
VMEM_LIMIT = 24 * 1024 * 1024
SIDES_AT_ONCE = 4
FINISH_AT_ONCE = 4
ADD_AT_ONCE = 2

F32 = jnp.float32
BF16 = jnp.bfloat16
NT = (((1,), (1,)), ((), ()))
TN = (((0,), (0,)), ((), ()))


def params():
    return pltpu.CompilerParams(vmem_limit_bytes=VMEM_LIMIT)


def whole(memory_space=pltpu.VMEM):
    return pl.BlockSpec(memory_space=memory_space)


def in_hbm(*values):
    return [pltpu.with_memory_space_constraint(value, pltpu.HBM) for value in values]


def lanes(step):
    return pl.ds(pl.multiple_of(step * LANES, LANES), LANES)


def sides_kernel(
    mask_hbm, flat_hbm, x_hbm, wag_hbm, wap_hbm, wbg_hbm, wbp_hbm,
    normed_ref, sides_ref,
    mask_ref, flat_ref, x_ref, w_ref, scratch, sems, few_sems,
):
    rows, columns, channels = x_ref.shape
    steps = columns // LANES
    few = [pltpu.make_async_copy(mask_hbm, mask_ref, few_sems.at[0])]
    few.append(pltpu.make_async_copy(flat_hbm, flat_ref, few_sems.at[1]))
    for n, w in enumerate((wag_hbm, wap_hbm, wbg_hbm, wbp_hbm)):
        few.append(pltpu.make_async_copy(w, w_ref.at[n], few_sems.at[2 + n]))

    def block(step):
        return pltpu.make_async_copy(x_hbm.at[:, lanes(step)], x_ref.at[:, lanes(step)], sems.at[step])

    block(0).start()
    for copy in few:
        copy.start()
    for step in range(1, steps):
        block(step).start()
    for copy in few:
        copy.wait()
    first = lax.axis_index(GROUP) * rows

    def one(step, slot):
        x = x_ref[:, lanes(step)].astype(F32).reshape(rows * LANES, channels)
        center = x - jnp.mean(x, axis=1, keepdims=True)
        second = jnp.mean(center * center, axis=1, keepdims=True)
        normed = (center * lax.rsqrt(second + EPS)).astype(BF16)
        normed_ref[:, lanes(step)] = normed.reshape(rows, LANES, channels)
        mask = mask_ref[step].astype(F32)
        w = jnp.concatenate([w_ref[n] for n in range(4)], axis=1)
        out = lax.dot_general(w, normed, (((0,), (1,)), ((), ())), preferred_element_type=F32)
        for side in range(2):
            gate = out[2 * side * LANES : (2 * side + 1) * LANES]
            proj = out[(2 * side + 1) * LANES : (2 * side + 2) * LANES]
            both = jax.nn.sigmoid(gate) * proj
            for k in range(rows):
                keep = mask * flat_ref[first + k].astype(F32)
                scratch[slot, side, pl.ds(k, LANES, stride=rows), :] = both[:, k * LANES : (k + 1) * LANES] * keep
            sides_ref[:, side, :, lanes(step)] = scratch[slot, side].reshape(LANES, rows, LANES).astype(BF16)

    def body(turn, carry):
        for slot in range(SIDES_AT_ONCE):
            block(turn * SIDES_AT_ONCE + slot).wait()
        for slot in range(SIDES_AT_ONCE):
            one(turn * SIDES_AT_ONCE + slot, slot)
        return carry

    lax.fori_loop(0, steps // SIDES_AT_ONCE, body, 0)


def make_sides(pair_rep, token_mask, w_a_gate, w_a_proj, w_b_gate, w_b_proj):
    rows, columns, channels = pair_rep.shape
    steps = columns // LANES
    return pl.pallas_call(
        sides_kernel,
        in_specs=[whole(pltpu.HBM)] * 7,
        out_specs=[whole(), whole()],
        out_shape=[
            jax.ShapeDtypeStruct(pair_rep.shape, BF16),
            jax.ShapeDtypeStruct((LANES, 2, rows, columns), BF16),
        ],
        scratch_shapes=[
            pltpu.VMEM((steps, 1, LANES), jnp.int32),
            pltpu.SMEM(token_mask.shape, jnp.int32),
            pltpu.VMEM(pair_rep.shape, BF16),
            pltpu.VMEM((4, channels, LANES), BF16),
            pltpu.VMEM((SIDES_AT_ONCE, 2, rows * LANES, LANES), F32),
            pltpu.SemaphoreType.DMA((steps,)),
            pltpu.SemaphoreType.DMA((6,)),
        ],
        compiler_params=params(),
        name="sides",
    )(
        *in_hbm(
            token_mask.reshape(steps, 1, LANES), token_mask, pair_rep, w_a_gate, w_a_proj, w_b_gate, w_b_proj
        )
    )


def product_kernel(sides_ref, out_ref):
    sources, _, rows, columns = sides_ref.shape
    depth = sources * rows
    block = 256

    def body(step, carry):
        here = pl.ds(pl.multiple_of(step * block, block), block)
        left = sides_ref[:, 0, :, here].reshape(depth, block)
        right = sides_ref[:, 1].reshape(depth, columns)
        prod = lax.dot_general(left, right, TN, preferred_element_type=F32)
        owners = block // rows
        out_ref[pl.ds(step * owners, owners)] = prod.reshape(owners, rows, columns).astype(BF16)
        return carry

    lax.fori_loop(0, columns // block, body, 0)


def make_product(sides):
    sources, _, rows, columns = sides.shape
    return pl.pallas_call(
        product_kernel,
        in_specs=[whole()],
        out_specs=whole(),
        out_shape=jax.ShapeDtypeStruct((columns // rows, rows, columns), BF16),
        compiler_params=params(),
        name="product",
    )(sides)


def finish_kernel(
    x_ref, base_ref, normed_ref, wg_ref, wo_ref, wd_ref,
    upd_hbm, own_ref, mirror_ref,
    upd_ref, scratch, wide, sems,
):
    rows, columns, channels = base_ref.shape
    owners = LANES // rows
    bins = wd_ref.shape[0]
    steps = columns // LANES

    def send(step):
        return pltpu.make_async_copy(upd_ref.at[:, lanes(step)], upd_hbm.at[:, lanes(step)], sems.at[step])

    def one(step, scratch_ref, wide_ref):
        here = lanes(step)
        x = x_ref[:, :, here].astype(F32)
        center = x - jnp.mean(x, axis=0, keepdims=True)
        second = jnp.mean(center * center, axis=0, keepdims=True)
        scratch_ref[...] = (center * lax.rsqrt(second + EPS)).reshape(scratch_ref.shape)
        tri = jnp.concatenate(
            [scratch_ref[pl.ds(r, LANES, stride=rows), :].astype(BF16) for r in range(rows)], axis=1
        )
        projected = lax.dot_general(tri, wo_ref[...], TN, preferred_element_type=F32)
        normed = normed_ref[:, here].reshape(rows * LANES, channels)
        gate = jax.nn.sigmoid(jnp.dot(normed, wg_ref[...], preferred_element_type=F32))
        base = base_ref[:, here].reshape(rows * LANES, channels).astype(F32)
        updated = (base + gate * projected).astype(BF16)
        upd_ref[:, here] = updated.reshape(rows, LANES, channels)
        wide_ref[...] = updated.astype(F32)
        weight = wd_ref[...]
        own = lax.dot_general(weight, updated, NT, preferred_element_type=F32)
        for r in range(rows):
            own_ref[r, :, here] = own[:, r * LANES : (r + 1) * LANES]
        zero = jnp.zeros_like(weight)
        twice = jnp.concatenate(
            [jnp.concatenate([weight, zero], axis=1), jnp.concatenate([zero, weight], axis=1)], axis=0
        )
        for pair in range(rows // 2):
            picks = []
            for s in (2 * pair, 2 * pair + 1):
                parts = [wide_ref[pl.ds(d * rows + s, rows, stride=LANES), :] for d in range(owners)]
                picks.append(jnp.concatenate(parts, axis=0).astype(BF16))
            mirror = lax.dot_general(jnp.concatenate(picks, axis=1), twice, NT, preferred_element_type=F32)
            mirror_ref[pl.ds(step * owners, owners), :, pair * 2 * bins : (pair + 1) * 2 * bins] = mirror.reshape(
                owners, rows, 2 * bins
            ).astype(BF16)

    def body(turn, carry):
        for slot in range(FINISH_AT_ONCE):
            one(turn * FINISH_AT_ONCE + slot, scratch.at[slot], wide.at[slot])
        for slot in range(FINISH_AT_ONCE):
            send(turn * FINISH_AT_ONCE + slot).start()
        return carry

    lax.fori_loop(0, steps // FINISH_AT_ONCE, body, 0)
    for step in range(steps):
        send(step).wait()


def make_finish(product, pair_rep, normed, w_gate, w_out, w_dist):
    rows, columns, channels = pair_rep.shape
    bins = w_dist.shape[1]
    return pl.pallas_call(
        finish_kernel,
        in_specs=[whole()] * 6,
        out_specs=[whole(pltpu.HBM), whole(), whole()],
        out_shape=[
            jax.ShapeDtypeStruct(pair_rep.shape, BF16),
            jax.ShapeDtypeStruct((rows, bins, columns), F32),
            jax.ShapeDtypeStruct((columns // rows, rows, rows * bins), BF16),
        ],
        scratch_shapes=[
            pltpu.VMEM(pair_rep.shape, BF16),
            pltpu.VMEM((FINISH_AT_ONCE, LANES * rows, LANES), F32),
            pltpu.VMEM((FINISH_AT_ONCE, rows * LANES, channels), F32),
            pltpu.SemaphoreType.DMA((columns // LANES,)),
        ],
        compiler_params=params(),
        name="finish",
    )(product, pair_rep, normed, w_gate, w_out, w_dist.T)


def add_kernel(own_ref, mirror_ref, out_hbm, out_ref, sems):
    rows, bins, columns = own_ref.shape
    owners = LANES // rows
    steps = columns // LANES

    def send(step):
        return pltpu.make_async_copy(out_ref.at[step], out_hbm.at[:, :, lanes(step)], sems.at[step])

    def one(step):
        mirror = mirror_ref[pl.ds(step * owners, owners)].reshape(LANES, rows * bins)
        turned = mirror.astype(F32).T
        flat_ref = out_ref.at[step].reshape(bins * rows, LANES)
        for r in range(rows):
            total = own_ref[r, :, lanes(step)] + turned[r * bins : (r + 1) * bins]
            flat_ref[pl.ds(r, bins, stride=rows), :] = total

    def body(turn, carry):
        for slot in range(ADD_AT_ONCE):
            one(turn * ADD_AT_ONCE + slot)
        for slot in range(ADD_AT_ONCE):
            send(turn * ADD_AT_ONCE + slot).start()
        return carry

    lax.fori_loop(0, steps // ADD_AT_ONCE, body, 0)
    for step in range(steps):
        send(step).wait()


def make_add(own, mirror):
    rows, bins, columns = own.shape
    steps = columns // LANES
    return pl.pallas_call(
        add_kernel,
        in_specs=[whole(), whole()],
        out_specs=whole(pltpu.HBM),
        out_shape=jax.ShapeDtypeStruct((bins, rows, columns), F32),
        scratch_shapes=[
            pltpu.VMEM((steps, bins, rows, LANES), F32),
            pltpu.SemaphoreType.DMA((steps,)),
        ],
        compiler_params=params(),
        name="add",
    )(own, mirror)


def exchange(values):
    return lax.all_to_all(values, GROUP, split_axis=0, concat_axis=0, tiled=True)


def local(pair_rep, token_mask, w_a_gate, w_a_proj, w_b_gate, w_b_proj, w_gate, w_out, w_dist):
    normed, sides = make_sides(pair_rep, token_mask, w_a_gate, w_a_proj, w_b_gate, w_b_proj)
    product = make_product(exchange(sides))
    updated, own, mirror = make_finish(exchange(product), pair_rep, normed, w_gate, w_out, w_dist)
    return (updated, make_add(own, exchange(mirror)))


def solution(mesh):
    in_specs = (P(("dp", "row", "chan"), None, None), P("dp"), P(), P(), P(), P(), P(), P(), P())
    out_specs = (P(("dp", "row", "chan"), None, None), P(None, ("dp", "row", "chan"), None))
    return jax.shard_map(local, mesh=mesh, in_specs=in_specs, out_specs=out_specs, check_vma=False)
```

```python
import jax
import jax.numpy as jnp
from jax import lax
from jax.experimental import pallas as pl
from jax.experimental.pallas import tpu as pltpu
from jax.sharding import PartitionSpec as P

EPS = 1e-05
PLACES = ("ylo", "z", "core", "chan")
GROUP = ("z", "chan", "core", "ylo")
GRID = (8, 4, 2, 2)
ROWS = 8
LANES = 128
VMEM_LIMIT = 24 * 1024 * 1024
SIDES_AT_ONCE = 4
FINISH_AT_ONCE = 4
ADD_AT_ONCE = 2

F32 = jnp.float32
BF16 = jnp.bfloat16
NT = (((1,), (1,)), ((), ()))
TN = (((0,), (0,)), ((), ()))


def params():
    return pltpu.CompilerParams(vmem_limit_bytes=VMEM_LIMIT)


def whole(memory_space=pltpu.VMEM):
    return pl.BlockSpec(memory_space=memory_space)


def in_hbm(*values):
    return [pltpu.with_memory_space_constraint(value, pltpu.HBM) for value in values]


def lanes(step):
    return pl.ds(pl.multiple_of(step * LANES, LANES), LANES)


def sides_kernel(
    mask_hbm, flat_hbm, x_hbm, wag_hbm, wap_hbm, wbg_hbm, wbp_hbm,
    normed_ref, sides_ref,
    mask_ref, flat_ref, x_ref, w_ref, scratch, sems, few_sems,
):
    rows, columns, channels = x_ref.shape
    steps = columns // LANES
    few = [pltpu.make_async_copy(mask_hbm, mask_ref, few_sems.at[0])]
    few.append(pltpu.make_async_copy(flat_hbm, flat_ref, few_sems.at[1]))
    for n, w in enumerate((wag_hbm, wap_hbm, wbg_hbm, wbp_hbm)):
        few.append(pltpu.make_async_copy(w, w_ref.at[n], few_sems.at[2 + n]))

    def block(step):
        return pltpu.make_async_copy(x_hbm.at[:, lanes(step)], x_ref.at[:, lanes(step)], sems.at[step])

    block(0).start()
    for copy in few:
        copy.start()
    for step in range(1, steps):
        block(step).start()
    for copy in few:
        copy.wait()
    first = lax.axis_index(PLACES) * rows

    def one(step, slot):
        x = x_ref[:, lanes(step)].astype(F32).reshape(rows * LANES, channels)
        center = x - jnp.mean(x, axis=1, keepdims=True)
        second = jnp.mean(center * center, axis=1, keepdims=True)
        normed = (center * lax.rsqrt(second + EPS)).astype(BF16)
        normed_ref[:, lanes(step)] = normed.reshape(rows, LANES, channels)
        mask = mask_ref[step].astype(F32)
        w = jnp.concatenate([w_ref[n] for n in range(4)], axis=1)
        out = lax.dot_general(w, normed, (((0,), (1,)), ((), ())), preferred_element_type=F32)
        for side in range(2):
            gate = out[2 * side * LANES : (2 * side + 1) * LANES]
            proj = out[(2 * side + 1) * LANES : (2 * side + 2) * LANES]
            both = jax.nn.sigmoid(gate) * proj
            for k in range(rows):
                keep = mask * flat_ref[first + k].astype(F32)
                scratch[slot, side, pl.ds(k, LANES, stride=rows), :] = both[:, k * LANES : (k + 1) * LANES] * keep
            sides_ref[:, side, :, lanes(step)] = scratch[slot, side].reshape(LANES, rows, LANES).astype(BF16)

    def body(turn, carry):
        for slot in range(SIDES_AT_ONCE):
            block(turn * SIDES_AT_ONCE + slot).wait()
        for slot in range(SIDES_AT_ONCE):
            one(turn * SIDES_AT_ONCE + slot, slot)
        return carry

    lax.fori_loop(0, steps // SIDES_AT_ONCE, body, 0)


def make_sides(pair_rep, token_mask, w_a_gate, w_a_proj, w_b_gate, w_b_proj):
    rows, columns, channels = pair_rep.shape
    steps = columns // LANES
    return pl.pallas_call(
        sides_kernel,
        in_specs=[whole(pltpu.HBM)] * 7,
        out_specs=[whole(), whole()],
        out_shape=[
            jax.ShapeDtypeStruct(pair_rep.shape, BF16),
            jax.ShapeDtypeStruct((LANES, 2, rows, columns), BF16),
        ],
        scratch_shapes=[
            pltpu.VMEM((steps, 1, LANES), jnp.int32),
            pltpu.SMEM(token_mask.shape, jnp.int32),
            pltpu.VMEM(pair_rep.shape, BF16),
            pltpu.VMEM((4, channels, LANES), BF16),
            pltpu.VMEM((SIDES_AT_ONCE, 2, rows * LANES, LANES), F32),
            pltpu.SemaphoreType.DMA((steps,)),
            pltpu.SemaphoreType.DMA((6,)),
        ],
        compiler_params=params(),
        name="sides",
    )(
        *in_hbm(
            token_mask.reshape(steps, 1, LANES), token_mask, pair_rep, w_a_gate, w_a_proj, w_b_gate, w_b_proj
        )
    )


def by_place(block, owners):
    across = GRID[1] * GRID[2]
    runs = GRID[0] * across // owners
    return lax.rem(block, runs) * (owners // across), block // runs


def product_kernel(sides_ref, out_ref):
    sources, _, rows, columns = sides_ref.shape
    depth = sources * rows
    block = 256
    owners = block // rows
    deep = owners // (GRID[1] * GRID[2])

    def body(step, carry):
        here = pl.ds(pl.multiple_of(step * block, block), block)
        left = sides_ref[:, 0, :, here].reshape(depth, block)
        right = sides_ref[:, 1].reshape(depth, columns)
        prod = lax.dot_general(left, right, TN, preferred_element_type=F32)
        prod = prod.reshape(deep, GRID[2], GRID[1], rows, columns).astype(BF16)
        z, ylo = by_place(step, owners)
        for core in range(GRID[2]):
            out_ref[pl.ds(z, deep), :, core, ylo] = prod[:, core]
        return carry

    lax.fori_loop(0, columns // block, body, 0)


def make_product(sides):
    sources, _, rows, columns = sides.shape
    product = pl.pallas_call(
        product_kernel,
        in_specs=[whole()],
        out_specs=whole(),
        out_shape=jax.ShapeDtypeStruct(GRID + (rows, columns), BF16),
        compiler_params=params(),
        name="product",
    )(sides)
    return product.reshape(columns // rows, rows, columns)


def finish_kernel(
    x_ref, base_ref, normed_ref, wg_ref, wo_ref, wd_ref,
    upd_hbm, own_ref, mirror_ref,
    upd_ref, scratch, wide, stage, sems,
):
    rows, columns, channels = base_ref.shape
    owners = LANES // rows
    bins = wd_ref.shape[0]
    steps = columns // LANES
    deep = owners // (GRID[1] * GRID[2])

    def send(step):
        return pltpu.make_async_copy(upd_ref.at[:, lanes(step)], upd_hbm.at[:, lanes(step)], sems.at[step])

    def one(step, scratch_ref, wide_ref, stage_ref):
        here = lanes(step)
        x = x_ref[:, :, here].astype(F32)
        center = x - jnp.mean(x, axis=0, keepdims=True)
        second = jnp.mean(center * center, axis=0, keepdims=True)
        scratch_ref[...] = (center * lax.rsqrt(second + EPS)).reshape(scratch_ref.shape)
        tri = jnp.concatenate(
            [scratch_ref[pl.ds(r, LANES, stride=rows), :].astype(BF16) for r in range(rows)], axis=1
        )
        projected = lax.dot_general(tri, wo_ref[...], TN, preferred_element_type=F32)
        normed = normed_ref[:, here].reshape(rows * LANES, channels)
        gate = jax.nn.sigmoid(jnp.dot(normed, wg_ref[...], preferred_element_type=F32))
        base = base_ref[:, here].reshape(rows * LANES, channels).astype(F32)
        updated = (base + gate * projected).astype(BF16)
        upd_ref[:, here] = updated.reshape(rows, LANES, channels)
        wide_ref[...] = updated.astype(F32)
        weight = wd_ref[...]
        own = lax.dot_general(weight, updated, NT, preferred_element_type=F32)
        for r in range(rows):
            own_ref[r, :, here] = own[:, r * LANES : (r + 1) * LANES]
        zero = jnp.zeros_like(weight)
        twice = jnp.concatenate(
            [jnp.concatenate([weight, zero], axis=1), jnp.concatenate([zero, weight], axis=1)], axis=0
        )
        z, ylo = by_place(step, owners)
        for pair in range(rows // 2):
            picks = [wide_ref[pl.ds(2 * pair + s, LANES, stride=rows), :].astype(BF16) for s in range(2)]
            mirror = lax.dot_general(jnp.concatenate(picks, axis=1), twice, NT, preferred_element_type=F32)
            for r in range(rows):
                stage_ref[pair, pl.ds(r, owners, stride=rows), :] = mirror[r * owners : (r + 1) * owners]
            turned = stage_ref[pair].reshape(deep, GRID[2], GRID[1], rows, 2 * bins).astype(BF16)
            for core in range(GRID[2]):
                mirror_ref[pl.ds(z, deep), :, core, ylo, :, pair * 2 * bins : (pair + 1) * 2 * bins] = turned[:, core]

    def body(turn, carry):
        for slot in range(FINISH_AT_ONCE):
            one(turn * FINISH_AT_ONCE + slot, scratch.at[slot], wide.at[slot], stage.at[slot])
        for slot in range(FINISH_AT_ONCE):
            send(turn * FINISH_AT_ONCE + slot).start()
        return carry

    lax.fori_loop(0, steps // FINISH_AT_ONCE, body, 0)
    for step in range(steps):
        send(step).wait()


def make_finish(product, pair_rep, normed, w_gate, w_out, w_dist):
    rows, columns, channels = pair_rep.shape
    bins = w_dist.shape[1]
    return pl.pallas_call(
        finish_kernel,
        in_specs=[whole()] * 6,
        out_specs=[whole(pltpu.HBM), whole(), whole()],
        out_shape=[
            jax.ShapeDtypeStruct(pair_rep.shape, BF16),
            jax.ShapeDtypeStruct((rows, bins, columns), F32),
            jax.ShapeDtypeStruct(GRID + (rows, rows * bins), BF16),
        ],
        scratch_shapes=[
            pltpu.VMEM(pair_rep.shape, BF16),
            pltpu.VMEM((FINISH_AT_ONCE, LANES * rows, LANES), F32),
            pltpu.VMEM((FINISH_AT_ONCE, rows * LANES, channels), F32),
            pltpu.VMEM((FINISH_AT_ONCE, rows // 2, LANES, LANES), F32),
            pltpu.SemaphoreType.DMA((columns // LANES,)),
        ],
        compiler_params=params(),
        name="finish",
    )(product, pair_rep, normed, w_gate, w_out, w_dist.T)


def add_kernel(own_ref, mirror_ref, out_hbm, out_ref, sems):
    rows, bins, columns = own_ref.shape
    owners = LANES // rows
    steps = columns // LANES
    deep = owners // (GRID[1] * GRID[2])

    def send(step):
        return pltpu.make_async_copy(out_ref.at[step], out_hbm.at[:, :, lanes(step)], sems.at[step])

    def one(step):
        z, ylo = by_place(step, owners)
        cores = [mirror_ref[pl.ds(z, deep), :, core, ylo] for core in range(GRID[2])]
        turned = jnp.stack(cores, axis=1).reshape(LANES, rows * bins).astype(F32).T
        flat_ref = out_ref.at[step].reshape(bins * rows, LANES)
        for r in range(rows):
            total = own_ref[r, :, lanes(step)] + turned[r * bins : (r + 1) * bins]
            flat_ref[pl.ds(r, bins, stride=rows), :] = total

    def body(turn, carry):
        for slot in range(ADD_AT_ONCE):
            one(turn * ADD_AT_ONCE + slot)
        for slot in range(ADD_AT_ONCE):
            send(turn * ADD_AT_ONCE + slot).start()
        return carry

    lax.fori_loop(0, steps // ADD_AT_ONCE, body, 0)
    for step in range(steps):
        send(step).wait()


def make_add(own, mirror):
    rows, bins, columns = own.shape
    steps = columns // LANES
    return pl.pallas_call(
        add_kernel,
        in_specs=[whole(), whole()],
        out_specs=whole(pltpu.HBM),
        out_shape=jax.ShapeDtypeStruct((bins, rows, columns), F32),
        scratch_shapes=[
            pltpu.VMEM((steps, bins, rows, LANES), F32),
            pltpu.SemaphoreType.DMA((steps,)),
        ],
        compiler_params=params(),
        name="add",
    )(own, mirror)


def exchange(values):
    return lax.all_to_all(values, GROUP, split_axis=0, concat_axis=0, tiled=True)


def local(pair_rep, token_mask, w_a_gate, w_a_proj, w_b_gate, w_b_proj, w_gate, w_out, w_dist):
    normed, sides = make_sides(pair_rep, token_mask, w_a_gate, w_a_proj, w_b_gate, w_b_proj)
    product = make_product(exchange(sides))
    updated, own, mirror = make_finish(exchange(product), pair_rep, normed, w_gate, w_out, w_dist)
    arrived = exchange(mirror.reshape((-1,) + mirror.shape[4:])).reshape(mirror.shape)
    return (updated, make_add(own, arrived))


def solution(mesh):
    z, chan, core, ylo = GRID
    split = jax.sharding.Mesh(mesh.devices.reshape(-1, ylo, z, core, chan), ("dp",) + PLACES)
    rows = ("dp",) + PLACES
    in_specs = (P(rows, None, None), P("dp"), P(), P(), P(), P(), P(), P(), P())
    out_specs = (P(rows, None, None), P(None, rows, None))
    return jax.shard_map(local, mesh=split, in_specs=in_specs, out_specs=out_specs, check_vma=False)
```

```python
import jax
import jax.numpy as jnp
from jax import lax
from jax.experimental import pallas as pl
from jax.experimental.pallas import tpu as pltpu
from jax.sharding import PartitionSpec as P

EPS = 1e-05
PLACES = ("ylo", "z", "core", "chan")
GROUP = ("z", "chan", "core", "ylo")
GRID = (8, 4, 2, 2)
ROWS = 8
LANES = 128
VMEM_LIMIT = 24 * 1024 * 1024
SIDES_AT_ONCE = 4
FINISH_AT_ONCE = 2
ADD_AT_ONCE = 1

F32 = jnp.float32
BF16 = jnp.bfloat16
NT = (((1,), (1,)), ((), ()))
TN = (((0,), (0,)), ((), ()))


def params():
    return pltpu.CompilerParams(vmem_limit_bytes=VMEM_LIMIT)


def whole(memory_space=pltpu.VMEM):
    return pl.BlockSpec(memory_space=memory_space)


def in_hbm(*values):
    return [pltpu.with_memory_space_constraint(value, pltpu.HBM) for value in values]


def lanes(step):
    return pl.ds(pl.multiple_of(step * LANES, LANES), LANES)


def sides_kernel(
    mask_hbm, flat_hbm, x_hbm, wag_hbm, wap_hbm, wbg_hbm, wbp_hbm,
    normed_ref, sides_ref,
    mask_ref, flat_ref, x_ref, w_ref, scratch, sems, few_sems,
):
    rows, columns, channels = x_ref.shape
    steps = columns // LANES
    few = [pltpu.make_async_copy(mask_hbm, mask_ref, few_sems.at[0])]
    few.append(pltpu.make_async_copy(flat_hbm, flat_ref, few_sems.at[1]))
    for n, w in enumerate((wag_hbm, wap_hbm, wbg_hbm, wbp_hbm)):
        few.append(pltpu.make_async_copy(w, w_ref.at[n], few_sems.at[2 + n]))

    def block(step):
        return pltpu.make_async_copy(x_hbm.at[:, lanes(step)], x_ref.at[:, lanes(step)], sems.at[step])

    block(0).start()
    for copy in few:
        copy.start()
    for step in range(1, steps):
        block(step).start()
    for copy in few:
        copy.wait()
    first = lax.axis_index(PLACES) * rows

    def one(step, slot):
        x = x_ref[:, lanes(step)].astype(F32).reshape(rows * LANES, channels)
        center = x - jnp.mean(x, axis=1, keepdims=True)
        second = jnp.mean(center * center, axis=1, keepdims=True)
        normed = (center * lax.rsqrt(second + EPS)).astype(BF16)
        normed_ref[:, lanes(step)] = normed.reshape(rows, LANES, channels)
        mask = mask_ref[step].astype(F32)
        w = jnp.concatenate([w_ref[n] for n in range(4)], axis=1)
        out = lax.dot_general(w, normed, (((0,), (1,)), ((), ())), preferred_element_type=F32)
        for side in range(2):
            gate = out[2 * side * LANES : (2 * side + 1) * LANES]
            proj = out[(2 * side + 1) * LANES : (2 * side + 2) * LANES]
            both = jax.nn.sigmoid(gate) * proj
            for k in range(rows):
                keep = mask * flat_ref[first + k].astype(F32)
                scratch[slot, side, pl.ds(k, LANES, stride=rows), :] = both[:, k * LANES : (k + 1) * LANES] * keep
            sides_ref[:, side, :, lanes(step)] = scratch[slot, side].reshape(LANES, rows, LANES).astype(BF16)

    def body(turn, carry):
        for slot in range(SIDES_AT_ONCE):
            block(turn * SIDES_AT_ONCE + slot).wait()
        for slot in range(SIDES_AT_ONCE):
            one(turn * SIDES_AT_ONCE + slot, slot)
        return carry

    lax.fori_loop(0, steps // SIDES_AT_ONCE, body, 0)


def make_sides(pair_rep, token_mask, w_a_gate, w_a_proj, w_b_gate, w_b_proj):
    rows, columns, channels = pair_rep.shape
    steps = columns // LANES
    return pl.pallas_call(
        sides_kernel,
        in_specs=[whole(pltpu.HBM)] * 7,
        out_specs=[whole(), whole()],
        out_shape=[
            jax.ShapeDtypeStruct(pair_rep.shape, BF16),
            jax.ShapeDtypeStruct((LANES, 2, rows, columns), BF16),
        ],
        scratch_shapes=[
            pltpu.VMEM((steps, 1, LANES), jnp.int32),
            pltpu.SMEM(token_mask.shape, jnp.int32),
            pltpu.VMEM(pair_rep.shape, BF16),
            pltpu.VMEM((4, channels, LANES), BF16),
            pltpu.VMEM((SIDES_AT_ONCE, 2, rows * LANES, LANES), F32),
            pltpu.SemaphoreType.DMA((steps,)),
            pltpu.SemaphoreType.DMA((6,)),
        ],
        compiler_params=params(),
        name="sides",
    )(
        *in_hbm(
            token_mask.reshape(steps, 1, LANES), token_mask, pair_rep, w_a_gate, w_a_proj, w_b_gate, w_b_proj
        )
    )


def by_place(block, owners):
    across = GRID[1] * GRID[2]
    runs = GRID[0] * across // owners
    return lax.rem(block, runs) * (owners // across), block // runs


def product_kernel(sides_ref, out_ref):
    sources, _, rows, columns = sides_ref.shape
    depth = sources * rows
    block = 256
    owners = block // rows
    deep = owners // (GRID[1] * GRID[2])

    def body(step, carry):
        here = pl.ds(pl.multiple_of(step * block, block), block)
        left = sides_ref[:, 0, :, here].reshape(depth, block)
        right = sides_ref[:, 1].reshape(depth, columns)
        prod = lax.dot_general(left, right, TN, preferred_element_type=F32)
        prod = prod.reshape(deep, GRID[2], GRID[1], rows, columns).astype(BF16)
        z, ylo = by_place(step, owners)
        for core in range(GRID[2]):
            out_ref[pl.ds(z, deep), :, core, ylo] = prod[:, core]
        return carry

    lax.fori_loop(0, columns // block, body, 0, unroll=True)


def make_product(sides):
    sources, _, rows, columns = sides.shape
    product = pl.pallas_call(
        product_kernel,
        in_specs=[whole()],
        out_specs=whole(),
        out_shape=jax.ShapeDtypeStruct(GRID + (rows, columns), BF16),
        compiler_params=params(),
        name="product",
    )(sides)
    return product.reshape(columns // rows, rows, columns)


def finish_kernel(
    x_ref, base_ref, normed_ref, wg_ref, wo_ref, wd_ref,
    upd_hbm, own_ref, mirror_ref,
    upd_ref, scratch, wide, stage, sems,
):
    rows, columns, channels = base_ref.shape
    owners = LANES // rows
    bins = wd_ref.shape[0]
    steps = columns // LANES
    deep = owners // (GRID[1] * GRID[2])

    def send(step):
        return pltpu.make_async_copy(upd_ref.at[:, lanes(step)], upd_hbm.at[:, lanes(step)], sems.at[step])

    def one(step, scratch_ref, wide_ref, stage_ref):
        here = lanes(step)
        x = x_ref[:, :, here].astype(F32)
        mean = jnp.mean(x, axis=0, keepdims=True)
        center = x - mean
        scale = lax.rsqrt(jnp.mean(center * center, axis=0, keepdims=True) + EPS)
        scratch_ref[...] = x.reshape(scratch_ref.shape)
        tri = jnp.concatenate(
            [
                ((scratch_ref[pl.ds(r, LANES, stride=rows), :] - mean[0, r : r + 1]) * scale[0, r : r + 1]).astype(BF16)
                for r in range(rows)
            ],
            axis=1,
        )
        projected = lax.dot_general(tri, wo_ref[...], TN, preferred_element_type=F32)
        normed = normed_ref[:, here].reshape(rows * LANES, channels)
        gate = jax.nn.sigmoid(jnp.dot(normed, wg_ref[...], preferred_element_type=F32))
        base = base_ref[:, here].reshape(rows * LANES, channels).astype(F32)
        updated = (base + gate * projected).astype(BF16)
        upd_ref[:, here] = updated.reshape(rows, LANES, channels)
        wide_ref[...] = updated.astype(F32)
        weight = wd_ref[...]
        own = lax.dot_general(weight, updated, NT, preferred_element_type=F32)
        for r in range(rows):
            own_ref[r, :, here] = own[:, r * LANES : (r + 1) * LANES]
        zero = jnp.zeros_like(weight)
        twice = jnp.concatenate(
            [jnp.concatenate([weight, zero], axis=1), jnp.concatenate([zero, weight], axis=1)], axis=0
        )
        z, ylo = by_place(step, owners)
        for pair in range(rows // 2):
            picks = [wide_ref[pl.ds(2 * pair + s, LANES, stride=rows), :].astype(BF16) for s in range(2)]
            mirror = lax.dot_general(jnp.concatenate(picks, axis=1), twice, NT, preferred_element_type=F32)
            for r in range(rows):
                stage_ref[pair, pl.ds(r, owners, stride=rows), :] = mirror[r * owners : (r + 1) * owners]
            turned = stage_ref[pair].reshape(deep, GRID[2], GRID[1], rows, 2 * bins).astype(BF16)
            for core in range(GRID[2]):
                mirror_ref[pl.ds(z, deep), :, core, ylo, :, pair * 2 * bins : (pair + 1) * 2 * bins] = turned[:, core]

    def body(turn, carry):
        for slot in range(FINISH_AT_ONCE):
            one(turn * FINISH_AT_ONCE + slot, scratch.at[slot], wide.at[slot], stage.at[slot])
        for slot in range(FINISH_AT_ONCE):
            send(turn * FINISH_AT_ONCE + slot).start()
        return carry

    lax.fori_loop(0, steps // FINISH_AT_ONCE, body, 0, unroll=True)
    for step in range(steps):
        send(step).wait()


def make_finish(product, pair_rep, normed, w_gate, w_out, w_dist):
    rows, columns, channels = pair_rep.shape
    bins = w_dist.shape[1]
    return pl.pallas_call(
        finish_kernel,
        in_specs=[whole()] * 6,
        out_specs=[whole(pltpu.HBM), whole(), whole()],
        out_shape=[
            jax.ShapeDtypeStruct(pair_rep.shape, BF16),
            jax.ShapeDtypeStruct((rows, bins, columns), F32),
            jax.ShapeDtypeStruct(GRID + (rows, rows * bins), BF16),
        ],
        scratch_shapes=[
            pltpu.VMEM(pair_rep.shape, BF16),
            pltpu.VMEM((FINISH_AT_ONCE, LANES * rows, LANES), F32),
            pltpu.VMEM((FINISH_AT_ONCE, rows * LANES, channels), F32),
            pltpu.VMEM((FINISH_AT_ONCE, rows // 2, LANES, LANES), F32),
            pltpu.SemaphoreType.DMA((columns // LANES,)),
        ],
        compiler_params=params(),
        name="finish",
    )(product, pair_rep, normed, w_gate, w_out, w_dist.T)


def add_kernel(own_ref, mirror_ref, out_hbm, out_ref, sems):
    rows, bins, columns = own_ref.shape
    owners = LANES // rows
    steps = columns // LANES
    deep = owners // (GRID[1] * GRID[2])

    def send(step):
        return pltpu.make_async_copy(out_ref.at[step], out_hbm.at[:, :, lanes(step)], sems.at[step])

    def one(step):
        z, ylo = by_place(step, owners)
        cores = [mirror_ref[pl.ds(z, deep), :, core, ylo] for core in range(GRID[2])]
        turned = jnp.stack(cores, axis=1).reshape(LANES, rows * bins).astype(F32).T
        flat_ref = out_ref.at[step].reshape(bins * rows, LANES)
        for r in range(rows):
            total = own_ref[r, :, lanes(step)] + turned[r * bins : (r + 1) * bins]
            flat_ref[pl.ds(r, bins, stride=rows), :] = total

    def body(turn, carry):
        for slot in range(ADD_AT_ONCE):
            one(turn * ADD_AT_ONCE + slot)
        for slot in range(ADD_AT_ONCE):
            send(turn * ADD_AT_ONCE + slot).start()
        return carry

    lax.fori_loop(0, steps // ADD_AT_ONCE, body, 0, unroll=True)
    for step in range(steps):
        send(step).wait()


def make_add(own, mirror):
    rows, bins, columns = own.shape
    steps = columns // LANES
    return pl.pallas_call(
        add_kernel,
        in_specs=[whole(), whole()],
        out_specs=whole(pltpu.HBM),
        out_shape=jax.ShapeDtypeStruct((bins, rows, columns), F32),
        scratch_shapes=[
            pltpu.VMEM((steps, bins, rows, LANES), F32),
            pltpu.SemaphoreType.DMA((steps,)),
        ],
        compiler_params=params(),
        name="add",
    )(own, mirror)


def exchange(values):
    return lax.all_to_all(values, GROUP, split_axis=0, concat_axis=0, tiled=True)


def local(pair_rep, token_mask, w_a_gate, w_a_proj, w_b_gate, w_b_proj, w_gate, w_out, w_dist):
    normed, sides = make_sides(pair_rep, token_mask, w_a_gate, w_a_proj, w_b_gate, w_b_proj)
    product = make_product(exchange(sides))
    updated, own, mirror = make_finish(exchange(product), pair_rep, normed, w_gate, w_out, w_dist)
    arrived = exchange(mirror.reshape((-1,) + mirror.shape[4:])).reshape(mirror.shape)
    return (updated, make_add(own, arrived))


def solution(mesh):
    z, chan, core, ylo = GRID
    split = jax.sharding.Mesh(mesh.devices.reshape(-1, ylo, z, core, chan), ("dp",) + PLACES)
    rows = ("dp",) + PLACES
    in_specs = (P(rows, None, None), P("dp"), P(), P(), P(), P(), P(), P(), P())
    out_specs = (P(rows, None, None), P(None, rows, None))
    return jax.shard_map(local, mesh=split, in_specs=in_specs, out_specs=out_specs, check_vma=False)
```

```python
import jax
import jax.numpy as jnp
from jax import lax
from jax.experimental import pallas as pl
from jax.experimental.pallas import tpu as pltpu
from jax.sharding import PartitionSpec as P

EPS = 1e-05
PLACES = ("ylo", "z", "core", "chan")
GROUP = ("z", "chan", "core", "ylo")
GRID = (8, 4, 2, 2)
ROWS = 8
LANES = 128
VMEM_LIMIT = 24 * 1024 * 1024
SIDES_AT_ONCE = (2, 6)
FINISH_AT_ONCE = 2
ADD_AT_ONCE = 1

F32 = jnp.float32
BF16 = jnp.bfloat16
NT = (((1,), (1,)), ((), ()))
TN = (((0,), (0,)), ((), ()))


def params():
    return pltpu.CompilerParams(vmem_limit_bytes=VMEM_LIMIT)


def whole(memory_space=pltpu.VMEM):
    return pl.BlockSpec(memory_space=memory_space)


def in_hbm(*values):
    return [pltpu.with_memory_space_constraint(value, pltpu.HBM) for value in values]


def lanes(step):
    return pl.ds(pl.multiple_of(step * LANES, LANES), LANES)


def sides_kernel(
    mask_hbm, flat_hbm, x_hbm, wag_hbm, wap_hbm, wbg_hbm, wbp_hbm,
    normed_ref, sides_ref,
    mask_ref, flat_ref, x_ref, w_ref, scratch, sems, few_sems,
):
    rows, columns, channels = x_ref.shape
    steps = columns // LANES
    few = [pltpu.make_async_copy(mask_hbm, mask_ref, few_sems.at[0])]
    few.append(pltpu.make_async_copy(flat_hbm, flat_ref, few_sems.at[1]))
    for n, w in enumerate((wag_hbm, wap_hbm, wbg_hbm, wbp_hbm)):
        few.append(pltpu.make_async_copy(w, w_ref.at[n], few_sems.at[2 + n]))

    def block(step):
        return pltpu.make_async_copy(x_hbm.at[:, lanes(step)], x_ref.at[:, lanes(step)], sems.at[step])

    block(0).start()
    for copy in few:
        copy.start()
    for step in range(1, steps):
        block(step).start()
    for copy in few:
        copy.wait()
    first = lax.axis_index(PLACES) * rows

    def one(step, slot):
        x = x_ref[:, lanes(step)].astype(F32).reshape(rows * LANES, channels)
        center = x - jnp.mean(x, axis=1, keepdims=True)
        second = jnp.mean(center * center, axis=1, keepdims=True)
        normed = (center * lax.rsqrt(second + EPS)).astype(BF16)
        normed_ref[:, lanes(step)] = normed.reshape(rows, LANES, channels)
        mask = mask_ref[step].astype(F32)
        w = jnp.concatenate([w_ref[n] for n in range(4)], axis=1)
        out = lax.dot_general(w, normed, (((0,), (1,)), ((), ())), preferred_element_type=F32)
        for side in range(2):
            gate = out[2 * side * LANES : (2 * side + 1) * LANES]
            proj = out[(2 * side + 1) * LANES : (2 * side + 2) * LANES]
            both = jax.nn.sigmoid(gate) * proj
            for k in range(rows):
                keep = mask * flat_ref[first + k].astype(F32)
                scratch[slot, side, pl.ds(k, LANES, stride=rows), :] = both[:, k * LANES : (k + 1) * LANES] * keep
            sides_ref[:, side, :, lanes(step)] = scratch[slot, side].reshape(LANES, rows, LANES).astype(BF16)

    at = 0
    for size in SIDES_AT_ONCE:
        for slot in range(size):
            block(at + slot).wait()
        for slot in range(size):
            one(at + slot, slot)
        at += size


def make_sides(pair_rep, token_mask, w_a_gate, w_a_proj, w_b_gate, w_b_proj):
    rows, columns, channels = pair_rep.shape
    steps = columns // LANES
    return pl.pallas_call(
        sides_kernel,
        in_specs=[whole(pltpu.HBM)] * 7,
        out_specs=[whole(), whole()],
        out_shape=[
            jax.ShapeDtypeStruct(pair_rep.shape, BF16),
            jax.ShapeDtypeStruct((LANES, 2, rows, columns), BF16),
        ],
        scratch_shapes=[
            pltpu.VMEM((steps, 1, LANES), jnp.int32),
            pltpu.SMEM(token_mask.shape, jnp.int32),
            pltpu.VMEM(pair_rep.shape, BF16),
            pltpu.VMEM((4, channels, LANES), BF16),
            pltpu.VMEM((max(SIDES_AT_ONCE), 2, rows * LANES, LANES), F32),
            pltpu.SemaphoreType.DMA((steps,)),
            pltpu.SemaphoreType.DMA((6,)),
        ],
        compiler_params=params(),
        name="sides",
    )(
        *in_hbm(
            token_mask.reshape(steps, 1, LANES), token_mask, pair_rep, w_a_gate, w_a_proj, w_b_gate, w_b_proj
        )
    )


def by_place(block, owners):
    across = GRID[1] * GRID[2]
    runs = GRID[0] * across // owners
    return lax.rem(block, runs) * (owners // across), block // runs


def product_kernel(sides_ref, out_ref):
    sources, _, rows, columns = sides_ref.shape
    depth = sources * rows
    block = 256
    owners = block // rows
    deep = owners // (GRID[1] * GRID[2])

    def body(step, carry):
        here = pl.ds(pl.multiple_of(step * block, block), block)
        left = sides_ref[:, 0, :, here].reshape(depth, block)
        right = sides_ref[:, 1].reshape(depth, columns)
        prod = lax.dot_general(left, right, TN, preferred_element_type=F32)
        prod = prod.reshape(deep, GRID[2], GRID[1], rows, columns).astype(BF16)
        z, ylo = by_place(step, owners)
        for core in range(GRID[2]):
            out_ref[pl.ds(z, deep), :, core, ylo] = prod[:, core]
        return carry

    lax.fori_loop(0, columns // block, body, 0, unroll=True)


def make_product(sides):
    sources, _, rows, columns = sides.shape
    product = pl.pallas_call(
        product_kernel,
        in_specs=[whole()],
        out_specs=whole(),
        out_shape=jax.ShapeDtypeStruct(GRID + (rows, columns), BF16),
        compiler_params=params(),
        name="product",
    )(sides)
    return product.reshape(columns // rows, rows, columns)


def finish_kernel(
    x_ref, base_ref, normed_ref, wg_ref, wo_ref, wd_ref,
    upd_hbm, own_ref, mirror_ref,
    upd_ref, scratch, wide, stage, sems,
):
    rows, columns, channels = base_ref.shape
    owners = LANES // rows
    bins = wd_ref.shape[0]
    steps = columns // LANES
    deep = owners // (GRID[1] * GRID[2])

    def send(step):
        return pltpu.make_async_copy(upd_ref.at[:, lanes(step)], upd_hbm.at[:, lanes(step)], sems.at[step])

    def one(step, scratch_ref, wide_ref, stage_ref):
        here = lanes(step)
        x = x_ref[:, :, here].astype(F32)
        mean = jnp.mean(x, axis=0, keepdims=True)
        center = x - mean
        scale = lax.rsqrt(jnp.mean(center * center, axis=0, keepdims=True) + EPS)
        scratch_ref[...] = x.reshape(scratch_ref.shape)
        tri = jnp.concatenate(
            [
                ((scratch_ref[pl.ds(r, LANES, stride=rows), :] - mean[0, r : r + 1]) * scale[0, r : r + 1]).astype(BF16)
                for r in range(rows)
            ],
            axis=1,
        )
        projected = lax.dot_general(tri, wo_ref[...], TN, preferred_element_type=F32)
        normed = normed_ref[:, here].reshape(rows * LANES, channels)
        gate = jax.nn.sigmoid(jnp.dot(normed, wg_ref[...], preferred_element_type=F32))
        base = base_ref[:, here].reshape(rows * LANES, channels).astype(F32)
        updated = (base + gate * projected).astype(BF16)
        upd_ref[:, here] = updated.reshape(rows, LANES, channels)
        wide_ref[...] = updated.astype(F32)
        weight = wd_ref[...]
        own = lax.dot_general(weight, updated, NT, preferred_element_type=F32)
        for r in range(rows):
            own_ref[r, :, here] = own[:, r * LANES : (r + 1) * LANES]
        zero = jnp.zeros_like(weight)
        twice = jnp.concatenate(
            [jnp.concatenate([weight, zero], axis=1), jnp.concatenate([zero, weight], axis=1)], axis=0
        )
        z, ylo = by_place(step, owners)
        for pair in range(rows // 2):
            picks = [wide_ref[pl.ds(2 * pair + s, LANES, stride=rows), :].astype(BF16) for s in range(2)]
            mirror = lax.dot_general(jnp.concatenate(picks, axis=1), twice, NT, preferred_element_type=F32)
            for r in range(rows):
                stage_ref[pair, pl.ds(r, owners, stride=rows), :] = mirror[r * owners : (r + 1) * owners]
            turned = stage_ref[pair].reshape(deep, GRID[2], GRID[1], rows, 2 * bins).astype(BF16)
            for core in range(GRID[2]):
                mirror_ref[pl.ds(z, deep), :, core, ylo, :, pair * 2 * bins : (pair + 1) * 2 * bins] = turned[:, core]

    def body(turn, carry):
        for slot in range(FINISH_AT_ONCE):
            one(turn * FINISH_AT_ONCE + slot, scratch.at[slot], wide.at[slot], stage.at[slot])
        for slot in range(FINISH_AT_ONCE):
            send(turn * FINISH_AT_ONCE + slot).start()
        return carry

    lax.fori_loop(0, steps // FINISH_AT_ONCE, body, 0, unroll=True)
    for step in range(steps):
        send(step).wait()


def make_finish(product, pair_rep, normed, w_gate, w_out, w_dist):
    rows, columns, channels = pair_rep.shape
    bins = w_dist.shape[1]
    return pl.pallas_call(
        finish_kernel,
        in_specs=[whole()] * 6,
        out_specs=[whole(pltpu.HBM), whole(), whole()],
        out_shape=[
            jax.ShapeDtypeStruct(pair_rep.shape, BF16),
            jax.ShapeDtypeStruct((rows, bins, columns), F32),
            jax.ShapeDtypeStruct(GRID + (rows, rows * bins), BF16),
        ],
        scratch_shapes=[
            pltpu.VMEM(pair_rep.shape, BF16),
            pltpu.VMEM((FINISH_AT_ONCE, LANES * rows, LANES), F32),
            pltpu.VMEM((FINISH_AT_ONCE, rows * LANES, channels), F32),
            pltpu.VMEM((FINISH_AT_ONCE, rows // 2, LANES, LANES), F32),
            pltpu.SemaphoreType.DMA((columns // LANES,)),
        ],
        compiler_params=params(),
        name="finish",
    )(product, pair_rep, normed, w_gate, w_out, w_dist.T)


def add_kernel(own_ref, mirror_ref, out_hbm, out_ref, sems):
    rows, bins, columns = own_ref.shape
    owners = LANES // rows
    steps = columns // LANES
    deep = owners // (GRID[1] * GRID[2])

    def send(step):
        return pltpu.make_async_copy(out_ref.at[step], out_hbm.at[:, :, lanes(step)], sems.at[step])

    def one(step):
        z, ylo = by_place(step, owners)
        cores = [mirror_ref[pl.ds(z, deep), :, core, ylo] for core in range(GRID[2])]
        turned = jnp.stack(cores, axis=1).reshape(LANES, rows * bins).astype(F32).T
        flat_ref = out_ref.at[step].reshape(bins * rows, LANES)
        for r in range(rows):
            total = own_ref[r, :, lanes(step)] + turned[r * bins : (r + 1) * bins]
            flat_ref[pl.ds(r, bins, stride=rows), :] = total

    def body(turn, carry):
        for slot in range(ADD_AT_ONCE):
            one(turn * ADD_AT_ONCE + slot)
        for slot in range(ADD_AT_ONCE):
            send(turn * ADD_AT_ONCE + slot).start()
        return carry

    lax.fori_loop(0, steps // ADD_AT_ONCE, body, 0, unroll=True)
    for step in range(steps):
        send(step).wait()


def make_add(own, mirror):
    rows, bins, columns = own.shape
    steps = columns // LANES
    return pl.pallas_call(
        add_kernel,
        in_specs=[whole(), whole()],
        out_specs=whole(pltpu.HBM),
        out_shape=jax.ShapeDtypeStruct((bins, rows, columns), F32),
        scratch_shapes=[
            pltpu.VMEM((steps, bins, rows, LANES), F32),
            pltpu.SemaphoreType.DMA((steps,)),
        ],
        compiler_params=params(),
        name="add",
    )(own, mirror)


def exchange(values):
    return lax.all_to_all(values, GROUP, split_axis=0, concat_axis=0, tiled=True)


def local(pair_rep, token_mask, w_a_gate, w_a_proj, w_b_gate, w_b_proj, w_gate, w_out, w_dist):
    normed, sides = make_sides(pair_rep, token_mask, w_a_gate, w_a_proj, w_b_gate, w_b_proj)
    product = make_product(exchange(sides))
    updated, own, mirror = make_finish(exchange(product), pair_rep, normed, w_gate, w_out, w_dist)
    arrived = exchange(mirror.reshape((-1,) + mirror.shape[4:])).reshape(mirror.shape)
    return (updated, make_add(own, arrived))


def solution(mesh):
    z, chan, core, ylo = GRID
    split = jax.sharding.Mesh(mesh.devices.reshape(-1, ylo, z, core, chan), ("dp",) + PLACES)
    rows = ("dp",) + PLACES
    in_specs = (P(rows, None, None), P("dp"), P(), P(), P(), P(), P(), P(), P())
    out_specs = (P(rows, None, None), P(None, rows, None))
    return jax.shard_map(local, mesh=split, in_specs=in_specs, out_specs=out_specs, check_vma=False)
```

```python
import jax
import jax.numpy as jnp
from jax import lax
from jax.experimental import pallas as pl
from jax.experimental.pallas import tpu as pltpu
from jax.sharding import PartitionSpec as P

EPS = 1e-05
PLACES = ("ylo", "z", "core", "chan")
GROUP = ("z", "chan", "core", "ylo")
GRID = (8, 4, 2, 2)
ROWS = 8
LANES = 128
VMEM_LIMIT = 24 * 1024 * 1024
SIDES_AT_ONCE = (2, 6)
FINISH_AT_ONCE = 2
ADD_AT_ONCE = 1

F32 = jnp.float32
BF16 = jnp.bfloat16
NT = (((1,), (1,)), ((), ()))
TN = (((0,), (0,)), ((), ()))


def params():
    return pltpu.CompilerParams(vmem_limit_bytes=VMEM_LIMIT)


def whole(memory_space=pltpu.VMEM):
    return pl.BlockSpec(memory_space=memory_space)


def in_hbm(*values):
    return [pltpu.with_memory_space_constraint(value, pltpu.HBM) for value in values]


def lanes(step):
    return pl.ds(pl.multiple_of(step * LANES, LANES), LANES)


def sides_kernel(
    mask_hbm, flat_hbm, x_hbm, wag_hbm, wap_hbm, wbg_hbm, wbp_hbm,
    normed_ref, sides_ref,
    mask_ref, flat_ref, x_ref, w_ref, scratch, sems, few_sems,
):
    rows, columns, channels = x_ref.shape
    steps = columns // LANES
    few = [pltpu.make_async_copy(mask_hbm, mask_ref, few_sems.at[0])]
    few.append(pltpu.make_async_copy(flat_hbm, flat_ref, few_sems.at[1]))
    for n, w in enumerate((wag_hbm, wap_hbm, wbg_hbm, wbp_hbm)):
        few.append(pltpu.make_async_copy(w, w_ref.at[n], few_sems.at[2 + n]))

    def block(step):
        return pltpu.make_async_copy(x_hbm.at[:, lanes(step)], x_ref.at[:, lanes(step)], sems.at[step])

    block(0).start()
    for copy in few:
        copy.start()
    for step in range(1, steps):
        block(step).start()
    for copy in few:
        copy.wait()
    first = lax.axis_index(PLACES) * rows

    def one(step, slot):
        x = x_ref[:, lanes(step)].astype(F32).reshape(rows * LANES, channels)
        center = x - jnp.mean(x, axis=1, keepdims=True)
        share = jnp.full((channels, LANES), 1 / channels, BF16)
        second = jnp.dot((center * center).astype(BF16), share, preferred_element_type=F32)
        normed = (center * lax.rsqrt(second + EPS)).astype(BF16)
        normed_ref[:, lanes(step)] = normed.reshape(rows, LANES, channels)
        mask = mask_ref[step].astype(F32)
        w = jnp.concatenate([w_ref[n] for n in range(4)], axis=1)
        out = lax.dot_general(w, normed, (((0,), (1,)), ((), ())), preferred_element_type=F32)
        for side in range(2):
            gate = out[2 * side * LANES : (2 * side + 1) * LANES]
            proj = out[(2 * side + 1) * LANES : (2 * side + 2) * LANES]
            both = jax.nn.sigmoid(gate) * proj
            for k in range(rows):
                keep = mask * flat_ref[first + k].astype(F32)
                scratch[slot, side, pl.ds(k, LANES, stride=rows), :] = both[:, k * LANES : (k + 1) * LANES] * keep
            sides_ref[:, side, :, lanes(step)] = scratch[slot, side].reshape(LANES, rows, LANES).astype(BF16)

    at = 0
    for size in SIDES_AT_ONCE:
        for slot in range(size):
            block(at + slot).wait()
        for slot in range(size):
            one(at + slot, slot)
        at += size


def make_sides(pair_rep, token_mask, w_a_gate, w_a_proj, w_b_gate, w_b_proj):
    rows, columns, channels = pair_rep.shape
    steps = columns // LANES
    return pl.pallas_call(
        sides_kernel,
        in_specs=[whole(pltpu.HBM)] * 7,
        out_specs=[whole(), whole()],
        out_shape=[
            jax.ShapeDtypeStruct(pair_rep.shape, BF16),
            jax.ShapeDtypeStruct((LANES, 2, rows, columns), BF16),
        ],
        scratch_shapes=[
            pltpu.VMEM((steps, 1, LANES), jnp.int32),
            pltpu.SMEM(token_mask.shape, jnp.int32),
            pltpu.VMEM(pair_rep.shape, BF16),
            pltpu.VMEM((4, channels, LANES), BF16),
            pltpu.VMEM((max(SIDES_AT_ONCE), 2, rows * LANES, LANES), F32),
            pltpu.SemaphoreType.DMA((steps,)),
            pltpu.SemaphoreType.DMA((6,)),
        ],
        compiler_params=params(),
        name="sides",
    )(
        *in_hbm(
            token_mask.reshape(steps, 1, LANES), token_mask, pair_rep, w_a_gate, w_a_proj, w_b_gate, w_b_proj
        )
    )


def by_place(block, owners):
    across = GRID[1] * GRID[2]
    runs = GRID[0] * across // owners
    return lax.rem(block, runs) * (owners // across), block // runs


def product_kernel(sides_ref, out_ref):
    sources, _, rows, columns = sides_ref.shape
    depth = sources * rows
    block = 256
    owners = block // rows
    deep = owners // (GRID[1] * GRID[2])

    def body(step, carry):
        here = pl.ds(pl.multiple_of(step * block, block), block)
        left = sides_ref[:, 0, :, here].reshape(depth, block)
        right = sides_ref[:, 1].reshape(depth, columns)
        prod = lax.dot_general(left, right, TN, preferred_element_type=F32)
        prod = prod.reshape(deep, GRID[2], GRID[1], rows, columns).astype(BF16)
        z, ylo = by_place(step, owners)
        for core in range(GRID[2]):
            out_ref[pl.ds(z, deep), :, core, ylo] = prod[:, core]
        return carry

    lax.fori_loop(0, columns // block, body, 0, unroll=True)


def make_product(sides):
    sources, _, rows, columns = sides.shape
    product = pl.pallas_call(
        product_kernel,
        in_specs=[whole()],
        out_specs=whole(),
        out_shape=jax.ShapeDtypeStruct(GRID + (rows, columns), BF16),
        compiler_params=params(),
        name="product",
    )(sides)
    return product.reshape(columns // rows, rows, columns)


def finish_kernel(
    x_ref, base_ref, normed_ref, wg_ref, wo_ref, wd_ref,
    upd_hbm, own_ref, mirror_ref,
    upd_ref, scratch, wide, stage, sems,
):
    rows, columns, channels = base_ref.shape
    owners = LANES // rows
    bins = wd_ref.shape[0]
    steps = columns // LANES
    deep = owners // (GRID[1] * GRID[2])

    def send(step):
        return pltpu.make_async_copy(upd_ref.at[:, lanes(step)], upd_hbm.at[:, lanes(step)], sems.at[step])

    def one(step, scratch_ref, wide_ref, stage_ref):
        here = lanes(step)
        x = x_ref[:, :, here].astype(F32)
        mean = jnp.mean(x, axis=0, keepdims=True)
        center = x - mean
        scale = lax.rsqrt(jnp.mean(center * center, axis=0, keepdims=True) + EPS)
        scratch_ref[...] = x.reshape(scratch_ref.shape)
        tri = jnp.concatenate(
            [
                ((scratch_ref[pl.ds(r, LANES, stride=rows), :] - mean[0, r : r + 1]) * scale[0, r : r + 1]).astype(BF16)
                for r in range(rows)
            ],
            axis=1,
        )
        projected = lax.dot_general(tri, wo_ref[...], TN, preferred_element_type=F32)
        normed = normed_ref[:, here].reshape(rows * LANES, channels)
        gate = jax.nn.sigmoid(jnp.dot(normed, wg_ref[...], preferred_element_type=F32))
        base = base_ref[:, here].reshape(rows * LANES, channels).astype(F32)
        updated = (base + gate * projected).astype(BF16)
        upd_ref[:, here] = updated.reshape(rows, LANES, channels)
        wide_ref[...] = updated.astype(F32)
        weight = wd_ref[...]
        own = lax.dot_general(weight, updated, NT, preferred_element_type=F32)
        for r in range(rows):
            own_ref[r, :, here] = own[:, r * LANES : (r + 1) * LANES]
        zero = jnp.zeros_like(weight)
        twice = jnp.concatenate(
            [jnp.concatenate([weight, zero], axis=1), jnp.concatenate([zero, weight], axis=1)], axis=0
        )
        z, ylo = by_place(step, owners)
        for pair in range(rows // 2):
            picks = [wide_ref[pl.ds(2 * pair + s, LANES, stride=rows), :].astype(BF16) for s in range(2)]
            mirror = lax.dot_general(jnp.concatenate(picks, axis=1), twice, NT, preferred_element_type=F32)
            for r in range(rows):
                stage_ref[pair, pl.ds(r, owners, stride=rows), :] = mirror[r * owners : (r + 1) * owners]
            turned = stage_ref[pair].reshape(deep, GRID[2], GRID[1], rows, 2 * bins).astype(BF16)
            for core in range(GRID[2]):
                mirror_ref[pl.ds(z, deep), :, core, ylo, :, pair * 2 * bins : (pair + 1) * 2 * bins] = turned[:, core]

    def body(turn, carry):
        for slot in range(FINISH_AT_ONCE):
            one(turn * FINISH_AT_ONCE + slot, scratch.at[slot], wide.at[slot], stage.at[slot])
        for slot in range(FINISH_AT_ONCE):
            send(turn * FINISH_AT_ONCE + slot).start()
        return carry

    lax.fori_loop(0, steps // FINISH_AT_ONCE, body, 0, unroll=True)
    for step in range(steps):
        send(step).wait()


def make_finish(product, pair_rep, normed, w_gate, w_out, w_dist):
    rows, columns, channels = pair_rep.shape
    bins = w_dist.shape[1]
    return pl.pallas_call(
        finish_kernel,
        in_specs=[whole()] * 6,
        out_specs=[whole(pltpu.HBM), whole(), whole()],
        out_shape=[
            jax.ShapeDtypeStruct(pair_rep.shape, BF16),
            jax.ShapeDtypeStruct((rows, bins, columns), F32),
            jax.ShapeDtypeStruct(GRID + (rows, rows * bins), BF16),
        ],
        scratch_shapes=[
            pltpu.VMEM(pair_rep.shape, BF16),
            pltpu.VMEM((FINISH_AT_ONCE, LANES * rows, LANES), F32),
            pltpu.VMEM((FINISH_AT_ONCE, rows * LANES, channels), F32),
            pltpu.VMEM((FINISH_AT_ONCE, rows // 2, LANES, LANES), F32),
            pltpu.SemaphoreType.DMA((columns // LANES,)),
        ],
        compiler_params=params(),
        name="finish",
    )(product, pair_rep, normed, w_gate, w_out, w_dist.T)


def add_kernel(own_ref, mirror_ref, out_hbm, out_ref, sems):
    rows, bins, columns = own_ref.shape
    owners = LANES // rows
    steps = columns // LANES
    deep = owners // (GRID[1] * GRID[2])

    def send(step):
        return pltpu.make_async_copy(out_ref.at[step], out_hbm.at[:, :, lanes(step)], sems.at[step])

    def one(step):
        z, ylo = by_place(step, owners)
        cores = [mirror_ref[pl.ds(z, deep), :, core, ylo] for core in range(GRID[2])]
        turned = jnp.stack(cores, axis=1).reshape(LANES, rows * bins).astype(F32).T
        flat_ref = out_ref.at[step].reshape(bins * rows, LANES)
        for r in range(rows):
            total = own_ref[r, :, lanes(step)] + turned[r * bins : (r + 1) * bins]
            flat_ref[pl.ds(r, bins, stride=rows), :] = total

    def body(turn, carry):
        for slot in range(ADD_AT_ONCE):
            one(turn * ADD_AT_ONCE + slot)
        for slot in range(ADD_AT_ONCE):
            send(turn * ADD_AT_ONCE + slot).start()
        return carry

    lax.fori_loop(0, steps // ADD_AT_ONCE, body, 0, unroll=True)
    for step in range(steps):
        send(step).wait()


def make_add(own, mirror):
    rows, bins, columns = own.shape
    steps = columns // LANES
    return pl.pallas_call(
        add_kernel,
        in_specs=[whole(), whole()],
        out_specs=whole(pltpu.HBM),
        out_shape=jax.ShapeDtypeStruct((bins, rows, columns), F32),
        scratch_shapes=[
            pltpu.VMEM((steps, bins, rows, LANES), F32),
            pltpu.SemaphoreType.DMA((steps,)),
        ],
        compiler_params=params(),
        name="add",
    )(own, mirror)


def exchange(values):
    return lax.all_to_all(values, GROUP, split_axis=0, concat_axis=0, tiled=True)


def local(pair_rep, token_mask, w_a_gate, w_a_proj, w_b_gate, w_b_proj, w_gate, w_out, w_dist):
    normed, sides = make_sides(pair_rep, token_mask, w_a_gate, w_a_proj, w_b_gate, w_b_proj)
    product = make_product(exchange(sides))
    updated, own, mirror = make_finish(exchange(product), pair_rep, normed, w_gate, w_out, w_dist)
    arrived = exchange(mirror.reshape((-1,) + mirror.shape[4:])).reshape(mirror.shape)
    return (updated, make_add(own, arrived))


def solution(mesh):
    z, chan, core, ylo = GRID
    split = jax.sharding.Mesh(mesh.devices.reshape(-1, ylo, z, core, chan), ("dp",) + PLACES)
    rows = ("dp",) + PLACES
    in_specs = (P(rows, None, None), P("dp"), P(), P(), P(), P(), P(), P(), P())
    out_specs = (P(rows, None, None), P(None, rows, None))
    return jax.shard_map(local, mesh=split, in_specs=in_specs, out_specs=out_specs, check_vma=False)
```
